32 devices in a mesh: row: 2 (over x), col: 16 (over z, y, core).
Axes of the slice: x: 2, y: 2, z: 4, core: 2. Of those that a mesh axis runs over, the one named last changes fastest.
Arguments:
- state_cov: float32 [8192, 8192], P('row', 'col'), may hold values from -6 to 6
- trans_first: float32 [64, 9, 128, 128], P('row'), may hold values from -0.1875 to 0.1875
- band_first: int32 [64, 9], P('row'), may hold values from 0 to 63, as said below
- trans_second: float32 [64, 9, 128, 128], P('col'), may hold values from -0.1875 to 0.1875
- band_second: int32 [64, 9], P('col'), may hold values from 0 to 63, as said below
- noise_cov: float32 [8192, 8192], P('col', 'row'), may hold values from -4 to 4
Outputs:
- forecast: float32 [8192, 8192], P('col', 'row')
The draws below stay inside these ranges and needn't reach their ends.
Inputs may be any that keep to these rules, and one draw needn't show every extreme that they name: `band_first`: row i lists 9 different block columns in increasing order, each within 8 of i; block rows 0 and 63 reach exactly 8 blocks away. `band_second`: row i lists 9 different block columns in increasing order, each within 8 of i; block rows 0 and 63 reach exactly 8 blocks away.
All inputs are finite; a program needn't handle non-finite values.
Results may differ from the reference program's by a relative error of at most 0.0003.
Values sent between devices are 32-bit elements; how exact they have to be, the bound alone decides.
No kernel may reach another device: no remote copies, remote signals or barrier semaphores. Data moves between devices by JAX's collectives and lax.ppermute only.
A program may use at most 256 MiB of HBM per device.

```python
import jax
import jax.numpy as jnp
from jax import lax

N = 8192
BS = 128
BAND = 9
REACH = 8
BLOCKS = 64


def band_table(key):
    window = 2 * REACH + 1
    ranking = jax.random.randint(key, (BLOCKS, window), 0, 1 << 20) * window + jnp.arange(window, dtype=jnp.int32)[None, :]
    position = jnp.arange(BLOCKS, dtype=jnp.int32)[:, None] - REACH + jnp.arange(window, dtype=jnp.int32)[None, :]
    inside = (position >= 0) & (position < BLOCKS)
    ranking = jnp.where(inside, ranking, -1)
    unused, chosen = lax.top_k(ranking, BAND)
    picked = jnp.take_along_axis(position, chosen, axis=1)
    return jnp.sort(picked, axis=1).astype(jnp.int32)


def draw_band_first(key, part):
    return band_table(jax.random.fold_in(key, 11))


def draw_band_second(key, part):
    return band_table(jax.random.fold_in(key, 23))


def steps_of(rng, dims, cuts, low, largest):
    gain, own = 1.0, jax.random.fold_in(rng, 6)
    for axis_at, shards_of in cuts:
        draws = jnp.exp(jax.random.uniform(jax.random.fold_in(own, axis_at), (shards_of,), jnp.float32, low / len(cuts), largest / len(cuts)))
        gain = gain * jnp.repeat(draws, dims[axis_at] // shards_of).reshape([-1 if axis == axis_at else 1 for axis in range(len(dims))])
    return gain


def centred(key, shape, width, reach, split=(), kind=jnp.bfloat16):
    factor_of = steps_of(key, shape, split, -0.22, 0.18) if split else 1.0
    values = jax.random.normal(key, shape, jnp.float32) * width * factor_of
    return jnp.minimum(jnp.maximum(values, -reach), reach).astype(kind)


def setup_inputs(seed: int = 0) -> dict:
    seeds = jax.random.split(jax.random.key(seed), 7)
    state_cov = centred(seeds[0], (N, N), 1.0, 6.0, ((0, 2), (1, 16)), jnp.float32)
    trans_first = centred(seeds[1], (BLOCKS, BAND, BS, BS), (BAND * BS) ** -0.5, 0.1875, ((0, 2),), jnp.float32)
    band_first = draw_band_first(jax.random.fold_in(seeds[6], 71), 0)
    trans_second = centred(seeds[3], (BLOCKS, BAND, BS, BS), (BAND * BS) ** -0.5, 0.1875, ((0, 16),), jnp.float32)
    band_second = draw_band_second(jax.random.fold_in(seeds[6], 71), 0)
    noise_cov = centred(seeds[5], (N, N), 0.5, 4.0, ((0, 16), (1, 2)), jnp.float32)
    return dict(state_cov=state_cov, trans_first=trans_first, band_first=band_first, trans_second=trans_second, band_second=band_second, noise_cov=noise_cov)


def band_product(blocks, offsets, field):
    block_tiles = field.reshape(BLOCKS, BS, field.shape[1])

    def single(pair):
        matrix_rows, columns = pair
        picked = jnp.take(block_tiles, columns.astype(jnp.int32), axis=0)
        return jnp.einsum("tik,tkc->ic", matrix_rows, picked, precision=lax.Precision.HIGHEST)

    result = lax.map(single, (blocks, offsets))
    return result.reshape(N, field.shape[1])


def reference(state_cov, trans_first, band_first, trans_second, band_second, noise_cov):
    advected = band_product(trans_first, band_first, state_cov)
    return band_product(trans_second, band_second, advected.T) + noise_cov
```

```python
import functools

import jax
import jax.numpy as jnp
from jax import lax
from jax.experimental import pallas as pl
from jax.experimental.pallas import tpu as pltpu
from jax.sharding import PartitionSpec as P

BAND = 9
REACH = 8
CHUNK = 2
FIRSTS = (0, 2, 6)
HALO = 4
FIRST = (1, 1, 2, 4, 4, 4)


def extended(block, sides, width):
    for axis, dim in sides:
        count = lax.axis_size(axis)
        forward = [(i, i + 1) for i in range(count - 1)]
        backward = [(target, source) for source, target in forward]
        low = lax.ppermute(
            lax.slice_in_dim(block, block.shape[dim] - width, None, axis=dim), axis, forward
        )
        high = lax.ppermute(lax.slice_in_dim(block, 0, width, axis=dim), axis, backward)
        block = jnp.concatenate([low, block, high], axis=dim)
    return block


def passed_along(x, axis, by):
    length = lax.axis_size(axis)
    pairs = [(i, i + by) for i in range(length) if 0 <= i + by < length]
    return lax.ppermute(x, axis, pairs)


def body(state_cov, trans_first, band_first, trans_second, band_second, noise_cov):
    rows_dev, cols_dev = state_cov.shape
    block_size = trans_first.shape[2]
    band_rows = trans_first.shape[0]
    padded = extended(state_cov, (("row", 0),), REACH * block_size)
    row_base = lax.axis_index("row") * band_rows - REACH
    row_tiles = padded.reshape(-1, block_size, cols_dev)
    picked = jnp.take(row_tiles, (band_first - row_base).reshape(-1), axis=0)
    picked = picked.reshape(band_rows, BAND, block_size, cols_dev)
    advected = jnp.einsum("btxy,btyc->bxc", trans_first, picked, precision=lax.Precision.HIGHEST)
    advected = advected.reshape(rows_dev, cols_dev)
    hop_count = -(-(REACH * block_size) // cols_dev)
    on_left = []
    on_right = []
    current_left = advected
    current_right = advected
    for distance in range(hop_count):
        current_left = passed_along(current_left, "col", 1)
        current_right = passed_along(current_right, "col", -1)
        on_left.append(current_left)
        on_right.append(current_right)
    widened = jnp.concatenate(on_left[::-1] + [advected] + on_right, axis=1)
    col_blocks = cols_dev // block_size
    col_base = lax.axis_index("col") * col_blocks - hop_count * col_blocks
    strips = widened.reshape(rows_dev, -1, block_size)
    gathered = jnp.take(strips, (band_second - col_base).reshape(-1), axis=1)
    gathered = gathered.reshape(rows_dev, col_blocks, BAND, block_size)
    product = jnp.einsum("jbtk,btik->jbi", gathered, trans_second, precision=lax.Precision.HIGHEST)
    product = product.reshape(rows_dev, cols_dev)
    return product.T + noise_cov


def split(x):
    high = x.astype(jnp.bfloat16)
    return high, (x - high.astype(jnp.float32)).astype(jnp.bfloat16)


def dot(a, b):
    return jnp.dot(a, b, preferred_element_type=jnp.float32)


def three(a_high, a_low, b_both, b_high):
    total = None
    for t in range(len(a_high)):
        part = dot(a_high[t], b_both[t])
        total = part if total is None else total + part
    for t in range(0, len(a_low), 2):
        low = jnp.concatenate(a_low[t : t + 2], axis=1)
        total = total + dot(low, jnp.concatenate(b_high[t : t + 2], axis=0))
    return total


def row_at(meta, rows, place):
    return jnp.where(meta[0] == 0, place, rows - 1 - place)


def edge_kernel(meta, state, after, out, tile, sems):
    rows = out.shape[0]
    first = jnp.where(meta[0] == 0, state.shape[0] - rows, 0)
    first = pl.ds(pl.multiple_of(first, rows), rows)
    take = pltpu.make_async_copy(state.at[first], tile, sems.at[0])
    take.start()
    take.wait()
    give = pltpu.make_async_copy(tile, out, sems.at[1])
    give.start()
    give.wait()


def first_kernel(start, count, beyond, others, *refs):
    band, meta, trans = refs[:3]
    states, halos = refs[3:5], refs[5:7]
    outs, (tiles, both, sems) = refs[7 + others : -3], refs[-3:]
    g = pl.program_id(0)
    bs = trans.shape[2]
    cols = tiles.shape[3]
    band_rows = states[0].shape[0] // bs
    core = meta[2]
    base = 2 * start + core - REACH
    slots = [core, 1 - core]

    def fetch(w, act):
        row = row_at(meta, band_rows, base + w)
        inside = (row >= 0) & (row < band_rows)

        @pl.when(inside)
        def _():
            at = pl.ds(pl.multiple_of(row * bs, bs), bs)
            for k in range(2):
                act(pltpu.make_async_copy(states[k].at[at], tiles.at[slots[k], w], sems.at[k, w]))

        if beyond:

            @pl.when(jnp.where(meta[0] == 0, row >= band_rows, row < 0))
            def _():
                at = jnp.where(row < 0, row + REACH, row - band_rows)
                at = pl.ds(pl.multiple_of(at * bs, bs), bs)
                for k in range(2):
                    act(pltpu.make_async_copy(halos[k].at[at], tiles.at[slots[k], w], sems.at[k, w]))

    def ready(w):
        fetch(w, lambda copy: copy.wait())
        for k in range(2):
            high, rest = split(tiles[k, w])
            both[w, :bs, k * cols : (k + 1) * cols] = high
            both[w, bs:, k * cols : (k + 1) * cols] = rest

    @pl.when(g == 0)
    def _():
        for w in range(tiles.shape[1]):
            fetch(w, lambda copy: copy.start())
        for w in range(2 * REACH - 1):
            ready(w)

    ready(2 * g + 2 * REACH - 1)
    ready(2 * g + 2 * REACH)
    mine = row_at(meta, band_rows, 2 * (start + g) + core)
    at = [row_at(meta, band_rows, band[mine, t] - meta[0] * band_rows) - base for t in range(BAND)]
    parts = [split(trans[0, t]) for t in range(BAND)]
    total = three(
        [jnp.concatenate([high, high], axis=1) for high, rest in parts],
        [rest for high, rest in parts],
        [both[k] for k in at],
        [both[k, :bs, :] for k in at],
    )
    for n in range(count):

        @pl.when(g == n)
        def _(n=n):
            outs[n][...] = total


def parts_kernel(own, other, out):
    blocks, _, bs, _ = own.shape
    for k, trans in enumerate((own, other)):
        for i in range(blocks):
            for t in range(BAND):
                high, rest = split(trans[i, t])
                out[k, i, t, :, :bs] = high
                out[k, i, t, :, bs:] = rest


def step_kernel(finish, merge, others, passed, rows, meta, band, other_band, parts, noise, *refs):
    refs = list(refs)
    take = lambda count: [refs.pop(0) for _ in range(count)]
    chunk = take(3) if finish is not None else []
    got = take(1) if merge is not None else []
    take(others)
    out = refs.pop(0) if finish is not None or merge is not None else None
    give = refs.pop(0) if finish is not None else None
    take(passed)
    side, core = meta[1], meta[2]
    ends = []

    def column(place, width):
        return pl.ds(pl.multiple_of(row_at(meta, rows, place) * width, width), width)

    def end(copy):
        copy.start()
        ends.append(copy)

    if finish is not None:
        tiles, both, weights, added, result, sems, weight_sems, out_sems = take(8)
        _, blocks, _, bs, _ = weights.shape
        reads = [
            pltpu.make_async_copy(chunk[k], tiles.at[k], sems.at[k]) for k in range(3)
        ]
        here = column(2 * finish + core, bs)
        reads.append(pltpu.make_async_copy(noise.at[:, here], added, sems.at[3]))
        loads = [
            [
                pltpu.make_async_copy(parts.at[k, i], weights.at[k, i], weight_sems.at[k, i])
                for i in range(blocks)
            ]
            for k in range(2)
        ]
        for copy in reads[:3] + loads[0] + loads[1] + reads[3:]:
            copy.start()
    if merge is not None:
        sum_tile, got_tile, merge_sems = take(3)
        there = column(2 * merge + 1 - core, got_tile.shape[1])
        merges = [
            pltpu.make_async_copy(got[0], got_tile, merge_sems.at[0]),
            pltpu.make_async_copy(noise.at[:, there], sum_tile, merge_sems.at[1]),
        ]
        for copy in merges:
            copy.start()
    if finish is not None:
        chip = tiles.shape[2] // bs
        for k, slot in enumerate((1, 2 - 2 * side, 2 * side)):
            reads[k].wait()
            for b in range(chip):
                high, rest = split(tiles[k, :, b * bs : (b + 1) * bs].T)
                both[slot * chip + b, :bs, :] = high
                both[slot * chip + b, bs:, :] = rest
        base = (meta[3] // 2 - 1) * chip
        for k, table in enumerate((band, other_band)):
            for i in range(blocks):
                loads[k][i].wait()
                at = [table[i, t] - base for t in range(BAND)]
                highs = [weights[k, i, t, :, :bs] for t in range(BAND)]
                result[k, i * bs : (i + 1) * bs, :] = three(
                    [jnp.concatenate([high, high], axis=1) for high in highs],
                    [weights[k, i, t, :, bs:] for t in range(BAND)],
                    [both[j] for j in at],
                    [both[j, :bs, :] for j in at],
                )
        reads[3].wait()
        result[0] = result[0] + added[...]
        end(pltpu.make_async_copy(result.at[1], give, out_sems.at[1]))
        end(pltpu.make_async_copy(result.at[0], out.at[:, here], out_sems.at[0]))
    if merge is not None:
        for copy in merges:
            copy.wait()
        sum_tile[...] = sum_tile[...] + got_tile[...]
        end(pltpu.make_async_copy(sum_tile, out.at[:, there], merge_sems.at[2]))
    for copy in ends:
        copy.wait()


ANY = pl.BlockSpec(memory_space=pl.ANY)
SMEM = pl.BlockSpec(memory_space=pltpu.SMEM)
VMEM = pl.BlockSpec(memory_space=pltpu.VMEM)
DMA = pltpu.SemaphoreType.DMA


def params():
    return pltpu.CompilerParams(vmem_limit_bytes=56 * 1024 * 1024)


def cost(rows, depth, cols, moved):
    return pl.CostEstimate(
        flops=6 * rows * depth * cols, bytes_accessed=4 * moved, transcendentals=0
    )


def edge_of(state, meta, bs, after):
    edge = (REACH * bs, state.shape[1])
    return pl.pallas_call(
        edge_kernel,
        out_shape=jax.ShapeDtypeStruct(edge, state.dtype),
        in_specs=[SMEM, ANY, ANY],
        out_specs=ANY,
        scratch_shapes=[pltpu.VMEM(edge, state.dtype), DMA((2,))],
        compiler_params=params(),
        name="edge",
    )(meta, state, after)


def first_stage(trans, band, meta, states, halos, start, count, beyond, after):
    band_rows, _, bs, _ = trans.shape
    cols = states[0].shape[1]
    window = 2 * count + 2 * REACH - 1

    def mine(g, band, meta):
        return (row_at(meta, band_rows, 2 * (start + g) + meta[2]), 0, 0, 0)

    return pl.pallas_call(
        functools.partial(first_kernel, start, count, beyond, len(after)),
        out_shape=[jax.ShapeDtypeStruct((bs, 2 * cols), jnp.float32)] * count,
        grid_spec=pltpu.PrefetchScalarGridSpec(
            num_scalar_prefetch=2,
            grid=(count,),
            in_specs=[pl.BlockSpec((1, BAND, bs, bs), mine)] + [ANY] * (4 + len(after)),
            out_specs=[pl.BlockSpec((bs, 2 * cols), lambda g, band, meta: (0, 0))] * count,
            scratch_shapes=[
                pltpu.VMEM((2, window, bs, cols), jnp.float32),
                pltpu.VMEM((window, 2 * bs, 2 * cols), jnp.bfloat16),
                DMA((2, window)),
            ],
        ),
        compiler_params=params(),
        cost_estimate=cost(count * bs, BAND * bs, 2 * cols, count * bs * (BAND * bs + 18 * cols)),
        name="first",
    )(band, meta, trans, *states, *halos, *after)


def parts_of(own, other, after):
    blocks, band, bs, _ = own.shape
    return pl.pallas_call(
        lambda own, other, after, out: parts_kernel(own, other, out),
        out_shape=jax.ShapeDtypeStruct((2, blocks, band, bs, 2 * bs), jnp.bfloat16),
        in_specs=[VMEM, VMEM, ANY],
        out_specs=VMEM,
        compiler_params=params(),
        cost_estimate=cost(1, 1, 1, 4 * own.size),
        name="parts",
    )(own, other, after)


def step(meta, bands, parts, noise, finish, merge, out, passed, after):
    _, blocks, _, bs, _ = parts.shape
    rows = noise.shape[1] // bs
    operands = [*finish[1:]] if finish else []
    operands += [merge[1]] if merge else []
    others = list(after)
    shapes, aliases = [], {}
    if finish or merge:
        if out is not None:
            aliases[5 + len(operands) + len(others)] = 0
            others.append(out)
        shapes.append(jax.ShapeDtypeStruct(noise.shape, noise.dtype))
    scratch = []
    column = (noise.shape[0], bs)
    if finish:
        shapes.append(jax.ShapeDtypeStruct(column, noise.dtype))
        tile = finish[1].shape
        scratch += [
            pltpu.VMEM((3, *tile), jnp.float32),
            pltpu.VMEM((3 * tile[1] // bs, 2 * bs, bs), jnp.bfloat16),
            pltpu.VMEM(parts.shape, parts.dtype),
            pltpu.VMEM(column, jnp.float32),
            pltpu.VMEM((2, *column), jnp.float32),
            DMA((4,)),
            DMA((2, blocks)),
            DMA((2,)),
        ]
    if merge:
        scratch += [pltpu.VMEM(column, jnp.float32)] * 2 + [DMA((3,))]
    for x in passed:
        aliases[5 + len(operands) + len(others)] = len(shapes)
        others.append(x)
        shapes.append(jax.ShapeDtypeStruct(x.shape, x.dtype))
    got = list(
        pl.pallas_call(
            functools.partial(
                step_kernel, finish[0] if finish else None, merge[0] if merge else None,
                len(others), len(passed), rows,
            ),
            out_shape=shapes,
            in_specs=[SMEM] * 3 + [ANY] * (2 + len(operands) + len(others)),
            out_specs=[ANY] * len(shapes),
            scratch_shapes=scratch,
            input_output_aliases=aliases,
            compiler_params=params(),
            cost_estimate=cost(2 * blocks * bs, BAND * bs, bs, parts.size),
            name="step",
        )(meta, *bands, parts, noise, *operands, *others)
    )
    out = got.pop(0) if finish or merge else out
    give = got.pop(0) if finish else None
    return out, give, got


def paired(state_cov, trans_first, band_first, trans_second, band_second, noise_cov):
    band_rows, bs = trans_first.shape[0], trans_first.shape[2]
    count = lax.axis_size("col")
    here = lax.axis_index("col")
    meta = jnp.stack([lax.axis_index("row"), here // 2 % 2, here % 2, here]).astype(jnp.int32)
    devices = range(count)
    to_other = [(c, c ^ 1) for c in devices]
    to_pair = [(c, c ^ 2) for c in devices]
    to_far = [(c, c + (4 if c & 2 == 0 else -4)) for c in devices]
    to_far = [(c, d) for c, d in to_far if 0 <= d < count]
    chunks = band_rows // 2
    swap = lambda x: lax.ppermute(x, "col", to_other)
    own, pair, far, gave = [], [], [], []

    states = (state_cov, swap(state_cov))
    halos = states
    out = None

    def first(after):
        start = len(own)
        size = FIRST[sum(1 for k in range(len(FIRST)) if sum(FIRST[: k + 1]) <= start)]
        beyond = 2 * (start + size) + REACH > band_rows
        own.extend(
            first_stage(
                trans_first, band_first, meta, states, halos if beyond else states,
                start, size, beyond, after,
            )
        )
        return [own[-1]]

    def send(x):
        pair.append(lax.ppermute(x, "col", to_pair))

    last = first([])
    send(own[0])
    edge = edge_of(state_cov, meta, bs, last[0])
    halo = lax.ppermute(edge, "row", [(0, 1), (1, 0)])
    last = first([edge])
    send(own[1])
    parts = parts_of(trans_second, swap(trans_second), last[0])
    bands = (band_second, swap(band_second))
    last = first([parts])
    for n in range(chunks + 3):
        after = list(last)
        if n == chunks - 1:
            after.append(pair[n])
        if n == HALO:
            after.append(halo)
        if n == HALO + 2:
            halos = (halo, swap(halo))
        done = n - 2
        finish = (done, own[done], pair[done], far[done]) if 0 <= done < chunks else None
        merge = (done - 1, gave[done - 1]) if done >= 1 else None
        passed = [pair[n]] if n + 1 < chunks else []
        if n + 2 < chunks:
            passed.append(own[n + 2])
        out, give, got = step(meta, bands, parts, noise_cov, finish, merge, out, passed, after)
        last = []
        if n + 1 < chunks:
            pair[n] = got[0]
            last = got[:1]
        if n + 2 < chunks:
            own[n + 2] = got[1]
            send(own[n + 2])
        if n < chunks:
            far.append(lax.ppermute(pair[n], "col", to_far))
        if finish:
            gave.append(swap(give))
        if n in FIRSTS:
            last = first(last)
    return out


def solution(mesh):
    def whole(state_cov, trans_first, band_first, trans_second, band_second, noise_cov):
        band_rows, bs = trans_first.shape[0], trans_first.shape[2]
        chip = 2 * state_cov.shape[1]
        fits = (
            mesh.shape["row"] == 2
            and mesh.shape["col"] % 4 == 0
            and band_rows >= 4 * REACH
            and chip == REACH * bs
            and band_rows == 2 * sum(FIRST)
        )
        do = paired if fits else body
        return do(state_cov, trans_first, band_first, trans_second, band_second, noise_cov)

    return jax.shard_map(
        whole,
        mesh=mesh,
        in_specs=(
            P("row", "col"),
            P("row", None, None, None),
            P("row", None),
            P("col", None, None, None),
            P("col", None),
            P("col", "row"),
        ),
        out_specs=P("col", "row"),
        check_vma=False,
    )
```

```python
import functools

import jax
import jax.numpy as jnp
from jax import lax
from jax.experimental import pallas as pl
from jax.experimental.pallas import tpu as pltpu
from jax.sharding import PartitionSpec as P

BAND = 9
REACH = 8
CHUNK = 2
FIRST = (1, 1, 2, 8, 4)
FIRSTS = (1, 6)
NEAR = 12
WIDTH = 256
FINISH = ((5, 0, 4), (9, 4, 4), (13, 8, 4), (15, 12, 2), (16, 14, 1), (17, 15, 1))
MERGE = (9, 13)
PARTS = 0
HALO = 3


def extended(block, sides, width):
    for axis, dim in sides:
        count = lax.axis_size(axis)
        forward = [(i, i + 1) for i in range(count - 1)]
        backward = [(target, source) for source, target in forward]
        low = lax.ppermute(
            lax.slice_in_dim(block, block.shape[dim] - width, None, axis=dim), axis, forward
        )
        high = lax.ppermute(lax.slice_in_dim(block, 0, width, axis=dim), axis, backward)
        block = jnp.concatenate([low, block, high], axis=dim)
    return block


def passed_along(x, axis, by):
    length = lax.axis_size(axis)
    pairs = [(i, i + by) for i in range(length) if 0 <= i + by < length]
    return lax.ppermute(x, axis, pairs)


def body(state_cov, trans_first, band_first, trans_second, band_second, noise_cov):
    rows_dev, cols_dev = state_cov.shape
    block_size = trans_first.shape[2]
    band_rows = trans_first.shape[0]
    padded = extended(state_cov, (("row", 0),), REACH * block_size)
    row_base = lax.axis_index("row") * band_rows - REACH
    row_tiles = padded.reshape(-1, block_size, cols_dev)
    picked = jnp.take(row_tiles, (band_first - row_base).reshape(-1), axis=0)
    picked = picked.reshape(band_rows, BAND, block_size, cols_dev)
    advected = jnp.einsum("btxy,btyc->bxc", trans_first, picked, precision=lax.Precision.HIGHEST)
    advected = advected.reshape(rows_dev, cols_dev)
    hop_count = -(-(REACH * block_size) // cols_dev)
    on_left = []
    on_right = []
    current_left = advected
    current_right = advected
    for distance in range(hop_count):
        current_left = passed_along(current_left, "col", 1)
        current_right = passed_along(current_right, "col", -1)
        on_left.append(current_left)
        on_right.append(current_right)
    widened = jnp.concatenate(on_left[::-1] + [advected] + on_right, axis=1)
    col_blocks = cols_dev // block_size
    col_base = lax.axis_index("col") * col_blocks - hop_count * col_blocks
    strips = widened.reshape(rows_dev, -1, block_size)
    gathered = jnp.take(strips, (band_second - col_base).reshape(-1), axis=1)
    gathered = gathered.reshape(rows_dev, col_blocks, BAND, block_size)
    product = jnp.einsum("jbtk,btik->jbi", gathered, trans_second, precision=lax.Precision.HIGHEST)
    product = product.reshape(rows_dev, cols_dev)
    return product.T + noise_cov


def split(x):
    high = x.astype(jnp.bfloat16)
    return high, (x - high.astype(jnp.float32)).astype(jnp.bfloat16)


def dot(a, b):
    return jnp.dot(a, b, preferred_element_type=jnp.float32)


def three(a_high, a_low, b_both, b_high):
    total = None
    for t in range(len(a_high)):
        part = dot(a_high[t], b_both[t])
        total = part if total is None else total + part
    for t in range(0, len(a_low), 2):
        low = jnp.concatenate(a_low[t : t + 2], axis=1)
        total = total + dot(low, jnp.concatenate(b_high[t : t + 2], axis=0))
    return total


def row_at(meta, rows, place):
    return jnp.where(meta[0] == 0, place, rows - 1 - place)


def rows_kernel(place, bs, meta, state, after, out, tile, sems):
    count = out.shape[0] // bs
    rows = state.shape[0] // bs
    first = jnp.where(meta[0] == 0, place, rows - place - count)
    copies = []
    for k in range(count):
        at = pl.ds(pl.multiple_of((first + k) * bs, bs), bs)
        to = pl.ds(k * bs, bs)
        take = pltpu.make_async_copy(state.at[at], tile.at[to], sems.at[0, k])
        take.start()
        copies.append((take, pltpu.make_async_copy(tile.at[to], out.at[to], sems.at[1, k])))
    for take, give in copies:
        take.wait()
        give.start()
    for take, give in copies:
        give.wait()


def first_kernel(start, count, beyond, others, *refs):
    band, meta, trans = refs[:3]
    state, near, whole, halos = refs[3], refs[4], refs[5], refs[6:8]
    outs, (tiles, both, result, sems) = refs[8 + others : -4], refs[-4:]
    g = pl.program_id(0)
    bs = trans.shape[2]
    cols = tiles.shape[3]
    band_rows = state.shape[0] // bs
    ahead = near.shape[0] // bs
    core = meta[2]
    base = 2 * start + core - REACH
    slots = [core, 1 - core]

    def fetch(w, act):
        row = row_at(meta, band_rows, base + w)
        inside = (row >= 0) & (row < band_rows)

        def copy(k, source, row):
            at = pl.ds(pl.multiple_of(row * bs, bs), bs)
            act(pltpu.make_async_copy(source.at[at], tiles.at[slots[k], w], sems.at[k, w]))

        @pl.when(inside)
        def _():
            copy(0, state, row)

        @pl.when(inside & (base + w < ahead))
        def _():
            copy(1, near, jnp.where(meta[0] == 0, row, row - (band_rows - ahead)))

        if 2 * (start + count) + REACH > ahead:

            @pl.when(inside & (base + w >= ahead))
            def _():
                copy(1, whole, row)

        if beyond:

            @pl.when(jnp.where(meta[0] == 0, row >= band_rows, row < 0))
            def _():
                for k in range(2):
                    copy(k, halos[k], jnp.where(row < 0, row + REACH, row - band_rows))

    def ready(w):
        fetch(w, lambda copy: copy.wait())
        for k in range(2):
            high, rest = split(tiles[k, w])
            both[w, :bs, k * cols : (k + 1) * cols] = high
            both[w, bs:, k * cols : (k + 1) * cols] = rest

    @pl.when(g == 0)
    def _():
        for w in range(tiles.shape[1]):
            fetch(w, lambda copy: copy.start())
        for w in range(2 * REACH - 1):
            ready(w)

    ready(2 * g + 2 * REACH - 1)
    ready(2 * g + 2 * REACH)
    mine = row_at(meta, band_rows, 2 * (start + g) + core)
    at = [row_at(meta, band_rows, band[mine, t] - meta[0] * band_rows) - base for t in range(BAND)]
    parts = [split(trans[0, t]) for t in range(BAND)]
    a_high = [jnp.concatenate([high, high], axis=1) for high, rest in parts]
    a_low = [rest for high, rest in parts]
    for c in range(0, 2 * cols, WIDTH):
        here = pl.ds(c, WIDTH)
        total = three(
            a_high, a_low, [both[k, :, here] for k in at], [both[k, :bs, here] for k in at]
        )
        result[here, :] = total.T
    for n in range(count):

        @pl.when(g == n)
        def _(n=n):
            outs[n][...] = result[...]


def parts_kernel(own, other, out):
    blocks, _, bs, _ = own.shape
    for k, trans in enumerate((own, other)):
        for i in range(blocks):
            for t in range(BAND):
                high, rest = split(trans[i, t])
                out[k, i, t, :, :bs] = high
                out[k, i, t, :, bs:] = rest


def step_kernel(halves, finish, merge, others, passed, rows, meta, band, other_band, parts, noise, *refs):
    refs = list(refs)
    take = lambda count: [refs.pop(0) for _ in range(count)]
    pieces = [take(3) for _ in finish]
    got = take(len(merge))
    take(others)
    out = refs.pop(0) if 0 in halves or merge else None
    give = refs.pop(0) if 1 in halves else None
    take(passed)
    side, core = meta[1], meta[2]
    ends = []

    def column(place, width):
        return pl.ds(pl.multiple_of(row_at(meta, rows, place) * width, width), width)

    def end(copy):
        copy.start()
        ends.append(copy)

    if finish:
        tiles, both, weights, added, result, sems, weight_sems, out_sems = take(8)
        _, blocks, _, bs, _ = weights.shape
        reads = [
            [pltpu.make_async_copy(pieces[f][k], tiles.at[f, k], sems.at[f, k]) for k in range(3)]
            for f in range(len(finish))
        ]
        here = [column(2 * n + core, bs) for n in finish]
        adds = [
            pltpu.make_async_copy(noise.at[:, here[f]], added.at[f], sems.at[f, 3])
            for f in range(len(finish))
            if 0 in halves
        ]
        loads = {
            k: [
                pltpu.make_async_copy(parts.at[k, i], weights.at[k, i], weight_sems.at[k, i])
                for i in range(blocks)
            ]
            for k in halves
        }
        for copy in sum(reads[:2] + [loads[k] for k in halves] + reads[2:], []) + adds:
            copy.start()
    merges = []
    for m, chunks in enumerate(merge):
        sums, got_tile, merge_sems = take(3)
        width = got_tile.shape[1] // len(chunks)
        there = [column(2 * n + 1 - core, width) for n in chunks]
        copies = [pltpu.make_async_copy(got[m], got_tile, merge_sems.at[0, 0])]
        for k in range(len(chunks)):
            copies.append(
                pltpu.make_async_copy(noise.at[:, there[k]], sums.at[k], merge_sems.at[1, k])
            )
        for copy in copies:
            copy.start()
        merges.append((copies, sums, got_tile, merge_sems, there, width))
    if finish:
        chip = tiles.shape[2] // bs
        base = (meta[3] // 2 - 1) * chip
        lanes = both.shape[3] // bs
        for first in range(0, len(finish), lanes):
            now = both.at[first // lanes % both.shape[0]]
            for f in range(first, first + lanes):
                to = slice((f - first) * bs, (f - first + 1) * bs)
                for k, slot in enumerate((1, 2 - 2 * side, 2 * side)):
                    reads[f][k].wait()
                    for b in range(chip):
                        high, rest = split(tiles[f, k, b * bs : (b + 1) * bs, :])
                        now[slot * chip + b, :bs, to] = high
                        now[slot * chip + b, bs:, to] = rest
            for k in halves:
                table = other_band if k else band
                for i in range(blocks):
                    if first == 0:
                        loads[k][i].wait()
                    at = [table[i, t] - base for t in range(BAND)]
                    highs = [weights[k, i, t, :, :bs] for t in range(BAND)]
                    result[k, i * bs : (i + 1) * bs, first * bs : (first + lanes) * bs] = three(
                        [jnp.concatenate([high, high], axis=1) for high in highs],
                        [weights[k, i, t, :, bs:] for t in range(BAND)],
                        [now[j] for j in at],
                        [now[j, :bs, :] for j in at],
                    )
        end(pltpu.make_async_copy(result.at[1], give, out_sems.at[0]))
        for f in range(len(adds)):
            adds[f].wait()
            added[f] = added[f] + result[0, :, f * bs : (f + 1) * bs]
            end(pltpu.make_async_copy(added.at[f], out.at[:, here[f]], out_sems.at[1 + f]))
    for copies, sums, got_tile, merge_sems, there, width in merges:
        for copy in copies:
            copy.wait()
        for k in range(len(there)):
            sums[k] = sums[k] + got_tile[:, k * width : (k + 1) * width]
            end(pltpu.make_async_copy(sums.at[k], out.at[:, there[k]], merge_sems.at[2, k]))
    for copy in ends:
        copy.wait()


ANY = pl.BlockSpec(memory_space=pl.ANY)
SMEM = pl.BlockSpec(memory_space=pltpu.SMEM)
VMEM = pl.BlockSpec(memory_space=pltpu.VMEM)
DMA = pltpu.SemaphoreType.DMA


def params():
    return pltpu.CompilerParams(vmem_limit_bytes=63 * 1024 * 1024)


def cost(rows, depth, cols, moved):
    return pl.CostEstimate(
        flops=6 * rows * depth * cols, bytes_accessed=4 * moved, transcendentals=0
    )


def rows_of(state, meta, bs, place, count, after):
    edge = (count * bs, state.shape[1])
    return pl.pallas_call(
        functools.partial(rows_kernel, place, bs),
        out_shape=jax.ShapeDtypeStruct(edge, state.dtype),
        in_specs=[SMEM, ANY, ANY],
        out_specs=ANY,
        scratch_shapes=[pltpu.VMEM(edge, state.dtype), DMA((2, count))],
        compiler_params=params(),
        name="rows",
    )(meta, state, after)


def first_stage(trans, band, meta, state, near, whole, halos, start, count, beyond, after):
    band_rows, _, bs, _ = trans.shape
    cols = state.shape[1]
    window = 2 * count + 2 * REACH - 1

    def mine(g, band, meta):
        return (row_at(meta, band_rows, 2 * (start + g) + meta[2]), 0, 0, 0)

    return pl.pallas_call(
        functools.partial(first_kernel, start, count, beyond, len(after)),
        out_shape=[jax.ShapeDtypeStruct((2 * cols, bs), jnp.float32)] * count,
        grid_spec=pltpu.PrefetchScalarGridSpec(
            num_scalar_prefetch=2,
            grid=(count,),
            in_specs=[pl.BlockSpec((1, BAND, bs, bs), mine)] + [ANY] * (5 + len(after)),
            out_specs=[pl.BlockSpec((2 * cols, bs), lambda g, band, meta: (0, 0))] * count,
            scratch_shapes=[
                pltpu.VMEM((2, window, bs, cols), jnp.float32),
                pltpu.VMEM((window, 2 * bs, 2 * cols), jnp.bfloat16),
                pltpu.VMEM((2 * cols, bs), jnp.float32),
                DMA((2, window)),
            ],
        ),
        compiler_params=params(),
        cost_estimate=cost(count * bs, BAND * bs, 2 * cols, count * bs * (BAND * bs + 18 * cols)),
        name="first",
    )(band, meta, trans, state, near, whole, *halos, *after)


def parts_of(own, other, after):
    blocks, band, bs, _ = own.shape
    return pl.pallas_call(
        lambda own, other, after, out: parts_kernel(own, other, out),
        out_shape=jax.ShapeDtypeStruct((2, blocks, band, bs, 2 * bs), jnp.bfloat16),
        in_specs=[VMEM, VMEM, ANY],
        out_specs=VMEM,
        compiler_params=params(),
        cost_estimate=cost(1, 1, 1, 4 * own.size),
        name="parts",
    )(own, other, after)


def step(meta, bands, parts, noise, halves, finish, merge, out, passed, after):
    blocks, bs = parts.shape[-4], parts.shape[-2]
    rows = noise.shape[1] // bs
    operands = [x for one in finish for x in one[1:]] + [one[1] for one in merge]
    others = list(after)
    shapes, aliases = [], {}
    if 0 in halves or merge:
        if out is not None:
            aliases[5 + len(operands) + len(others)] = 0
            others.append(out)
        shapes.append(jax.ShapeDtypeStruct(noise.shape, noise.dtype))
    scratch = []
    column = (noise.shape[0], bs)
    if finish:
        count = len(finish)
        wide = (noise.shape[0], count * bs)
        if 1 in halves:
            shapes.append(jax.ShapeDtypeStruct(wide, noise.dtype))
        tile = finish[0][1].shape
        scratch += [
            pltpu.VMEM((count, 3, *tile), jnp.float32),
            pltpu.VMEM((-(-count // 2), 3 * tile[0] // bs, 2 * bs, min(count, 2) * bs), jnp.bfloat16),
            pltpu.VMEM(parts.shape, parts.dtype),
            pltpu.VMEM((count, *column), jnp.float32),
            pltpu.VMEM((2, *wide), jnp.float32),
            DMA((count, 4)),
            DMA((2, blocks)),
            DMA((1 + count,)),
        ]
    for chunks, got in merge:
        count = len(chunks)
        scratch += [
            pltpu.VMEM((count, *column), jnp.float32),
            pltpu.VMEM(got.shape, jnp.float32),
            DMA((3, count)),
        ]
    for x in passed:
        aliases[5 + len(operands) + len(others)] = len(shapes)
        others.append(x)
        shapes.append(jax.ShapeDtypeStruct(x.shape, x.dtype))
    got = list(
        pl.pallas_call(
            functools.partial(
                step_kernel, halves, [one[0] for one in finish], [one[0] for one in merge],
                len(others), len(passed), rows,
            ),
            out_shape=shapes,
            in_specs=[SMEM] * 3 + [ANY] * (2 + len(operands) + len(others)),
            out_specs=[ANY] * len(shapes),
            scratch_shapes=scratch,
            input_output_aliases=aliases,
            compiler_params=params(),
            cost_estimate=cost(2 * blocks * bs, BAND * bs, bs, parts.size),
            name="step",
        )(meta, *bands, parts, noise, *operands, *others)
    )
    out = got.pop(0) if 0 in halves or merge else out
    give = got.pop(0) if 1 in halves else None
    return out, give, got


def paired(state_cov, trans_first, band_first, trans_second, band_second, noise_cov):
    band_rows, bs = trans_first.shape[0], trans_first.shape[2]
    count = lax.axis_size("col")
    here = lax.axis_index("col")
    meta = jnp.stack([lax.axis_index("row"), here // 2 % 2, here % 2, here]).astype(jnp.int32)
    devices = range(count)
    to_other = [(c, c ^ 1) for c in devices]
    to_pair = [(c, c ^ 2) for c in devices]
    to_far = [(c, c + (4 if c & 2 == 0 else -4)) for c in devices]
    to_far = [(c, d) for c, d in to_far if 0 <= d < count]
    chunks = band_rows // 2
    swap = lambda x: lax.ppermute(x, "col", to_other)
    own, pair, far = [], [], []
    halos = (state_cov, state_cov)
    out = None

    def first(after):
        start = len(own)
        size = FIRST[sum(1 for k in range(len(FIRST)) if sum(FIRST[: k + 1]) <= start)]
        beyond = 2 * (start + size) + REACH > band_rows
        own.extend(
            first_stage(
                trans_first, band_first, meta, state_cov, near, whole if start > 1 else near, halos,
                start, size, beyond, after,
            )
        )
        return [own[-1]]

    def send(x):
        pair.append(lax.ppermute(x, "col", to_pair))

    rows = lambda place, size, after: rows_of(state_cov, meta, bs, place, size, after)
    ahead = rows(0, NEAR, meta)
    near = swap(ahead)
    edge = rows(band_rows - REACH, REACH, ahead)
    halo = lax.ppermute(edge, "row", [(0, 1), (1, 0)])
    tile, near = lax.optimization_barrier((state_cov, near))
    whole = swap(tile)
    bands = (band_second, swap(band_second))
    last = first([edge, bands[1]])
    send(own[0])
    trans, last[0] = lax.optimization_barrier((trans_second, last[0]))
    last = first(last)
    send(own[1])
    other_trans = swap(trans)
    last = first(last)
    gave, merge = [], []
    parts = trans_second

    def finish(first_chunk, size):
        nonlocal out, last, merge
        done = tuple(range(first_chunk, first_chunk + size))
        out, give, _ = step(
            meta, bands, parts, noise_cov, (1, 0),
            [(m, own[m], pair[m], far[m]) for m in done], merge, out, [], [x for x in last if x is not out],
        )
        gave.append((done, swap(give)))
        merge = []
        last = [out]

    for n in range(chunks + 2):
        if n < chunks:
            after = [far[n - 2]] if n >= 2 else []
            passed = [pair[n]]
            if n + 2 < chunks:
                passed.append(own[n + 2])
            if n == HALO:
                passed.append(halo)
            _, _, got = step(
                meta, bands, parts, noise_cov, (), [], [], None, passed, [*last, *after]
            )
            pair[n], last = got[0], got[:1]
            if n == HALO:
                halos = (got[-1], swap(got[-1]))
            if n + 2 < chunks:
                own[n + 2] = got[1]
                send(own[n + 2])
            far.append(lax.ppermute(pair[n], "col", to_far))
            if n in FIRSTS:
                last = first(last)
            if n == PARTS:
                parts = parts_of(trans_second, other_trans, last[0])
                last = [parts]
        for at, first_chunk, size in FINISH:
            if at == n:
                if n in MERGE:
                    merge, gave = gave, []
                finish(first_chunk, size)
    out, _, _ = step(meta, bands, parts, noise_cov, (), [], gave, out, [], [])
    return out


def solution(mesh):
    def whole(state_cov, trans_first, band_first, trans_second, band_second, noise_cov):
        band_rows, bs = trans_first.shape[0], trans_first.shape[2]
        chip = 2 * state_cov.shape[1]
        fits = (
            mesh.shape["row"] == 2
            and mesh.shape["col"] % 4 == 0
            and band_rows >= 4 * REACH
            and chip == REACH * bs
            and band_rows == 2 * sum(FIRST) == 2 * sum(size for _, _, size in FINISH)
        )
        do = paired if fits else body
        return do(state_cov, trans_first, band_first, trans_second, band_second, noise_cov)

    return jax.shard_map(
        whole,
        mesh=mesh,
        in_specs=(
            P("row", "col"),
            P("row", None, None, None),
            P("row", None),
            P("col", None, None, None),
            P("col", None),
            P("col", "row"),
        ),
        out_specs=P("col", "row"),
        check_vma=False,
    )
```

```python
import functools

import jax
import jax.numpy as jnp
from jax import lax
from jax.experimental import pallas as pl
from jax.experimental.pallas import tpu as pltpu
from jax.sharding import PartitionSpec as P

BAND = 9
REACH = 8
CHUNK = 2
FIRST = (1, 1, 2, 4, 4, 4)
FIRSTS = (1, 3, 7)
NEAR = 12
WIDTH = 256
FINISH = ((5, 0, 4), (9, 4, 4), (12, 8, 2), (14, 10, 2), (15, 12, 2), (16, 14, 1), (17, 15, 1))
MERGE = (9, 14, 17)
PARTS = -1
HALO = 3


def extended(block, sides, width):
    for axis, dim in sides:
        count = lax.axis_size(axis)
        forward = [(i, i + 1) for i in range(count - 1)]
        backward = [(target, source) for source, target in forward]
        low = lax.ppermute(
            lax.slice_in_dim(block, block.shape[dim] - width, None, axis=dim), axis, forward
        )
        high = lax.ppermute(lax.slice_in_dim(block, 0, width, axis=dim), axis, backward)
        block = jnp.concatenate([low, block, high], axis=dim)
    return block


def passed_along(x, axis, by):
    length = lax.axis_size(axis)
    pairs = [(i, i + by) for i in range(length) if 0 <= i + by < length]
    return lax.ppermute(x, axis, pairs)


def body(state_cov, trans_first, band_first, trans_second, band_second, noise_cov):
    rows_dev, cols_dev = state_cov.shape
    block_size = trans_first.shape[2]
    band_rows = trans_first.shape[0]
    padded = extended(state_cov, (("row", 0),), REACH * block_size)
    row_base = lax.axis_index("row") * band_rows - REACH
    row_tiles = padded.reshape(-1, block_size, cols_dev)
    picked = jnp.take(row_tiles, (band_first - row_base).reshape(-1), axis=0)
    picked = picked.reshape(band_rows, BAND, block_size, cols_dev)
    advected = jnp.einsum("btxy,btyc->bxc", trans_first, picked, precision=lax.Precision.HIGHEST)
    advected = advected.reshape(rows_dev, cols_dev)
    hop_count = -(-(REACH * block_size) // cols_dev)
    on_left = []
    on_right = []
    current_left = advected
    current_right = advected
    for distance in range(hop_count):
        current_left = passed_along(current_left, "col", 1)
        current_right = passed_along(current_right, "col", -1)
        on_left.append(current_left)
        on_right.append(current_right)
    widened = jnp.concatenate(on_left[::-1] + [advected] + on_right, axis=1)
    col_blocks = cols_dev // block_size
    col_base = lax.axis_index("col") * col_blocks - hop_count * col_blocks
    strips = widened.reshape(rows_dev, -1, block_size)
    gathered = jnp.take(strips, (band_second - col_base).reshape(-1), axis=1)
    gathered = gathered.reshape(rows_dev, col_blocks, BAND, block_size)
    product = jnp.einsum("jbtk,btik->jbi", gathered, trans_second, precision=lax.Precision.HIGHEST)
    product = product.reshape(rows_dev, cols_dev)
    return product.T + noise_cov


def split(x):
    high = x.astype(jnp.bfloat16)
    return high, (x - high.astype(jnp.float32)).astype(jnp.bfloat16)


def dot(a, b):
    return jnp.dot(a, b, preferred_element_type=jnp.float32)


def three(a_high, a_low, b_both, b_high):
    total = None
    for t in range(len(a_high)):
        part = dot(a_high[t], b_both[t])
        total = part if total is None else total + part
    for t in range(0, len(a_low), 2):
        low = jnp.concatenate(a_low[t : t + 2], axis=1)
        total = total + dot(low, jnp.concatenate(b_high[t : t + 2], axis=0))
    return total


def row_at(meta, rows, place):
    return jnp.where(meta[0] == 0, place, rows - 1 - place)


def rows_kernel(place, bs, meta, state, after, out, tile, sems):
    count = out.shape[0] // bs
    rows = state.shape[0] // bs
    first = jnp.where(meta[0] == 0, place, rows - place - count)
    copies = []
    for k in range(count):
        at = pl.ds(pl.multiple_of((first + k) * bs, bs), bs)
        to = pl.ds(k * bs, bs)
        take = pltpu.make_async_copy(state.at[at], tile.at[to], sems.at[0, k])
        take.start()
        copies.append((take, pltpu.make_async_copy(tile.at[to], out.at[to], sems.at[1, k])))
    for take, give in copies:
        take.wait()
        give.start()
    for take, give in copies:
        give.wait()


def first_kernel(start, count, beyond, others, *refs):
    band, meta, trans = refs[:3]
    state, near, whole, halos = refs[3], refs[4], refs[5], refs[6:8]
    outs, (tiles, both, result, sems) = refs[8 + others : -4], refs[-4:]
    g = pl.program_id(0)
    bs = trans.shape[2]
    cols = tiles.shape[3]
    band_rows = state.shape[0] // bs
    ahead = near.shape[0] // bs
    core = meta[2]
    base = 2 * start + core - REACH
    slots = [core, 1 - core]

    def fetch(w, act):
        row = row_at(meta, band_rows, base + w)
        inside = (row >= 0) & (row < band_rows)

        def copy(k, source, row):
            at = pl.ds(pl.multiple_of(row * bs, bs), bs)
            act(pltpu.make_async_copy(source.at[at], tiles.at[slots[k], w], sems.at[k, w]))

        @pl.when(inside)
        def _():
            copy(0, state, row)

        @pl.when(inside & (base + w < ahead))
        def _():
            copy(1, near, jnp.where(meta[0] == 0, row, row - (band_rows - ahead)))

        if 2 * (start + count) + REACH > ahead:

            @pl.when(inside & (base + w >= ahead))
            def _():
                copy(1, whole, row)

        if beyond:

            @pl.when(jnp.where(meta[0] == 0, row >= band_rows, row < 0))
            def _():
                for k in range(2):
                    copy(k, halos[k], jnp.where(row < 0, row + REACH, row - band_rows))

    def ready(w):
        fetch(w, lambda copy: copy.wait())
        for k in range(2):
            high, rest = split(tiles[k, w])
            both[w, :bs, k * cols : (k + 1) * cols] = high
            both[w, bs:, k * cols : (k + 1) * cols] = rest

    @pl.when(g == 0)
    def _():
        for w in range(tiles.shape[1]):
            fetch(w, lambda copy: copy.start())
        for w in range(2 * REACH - 1):
            ready(w)

    ready(2 * g + 2 * REACH - 1)
    ready(2 * g + 2 * REACH)
    mine = row_at(meta, band_rows, 2 * (start + g) + core)
    at = [row_at(meta, band_rows, band[mine, t] - meta[0] * band_rows) - base for t in range(BAND)]
    parts = [split(trans[0, t]) for t in range(BAND)]
    a_high = [jnp.concatenate([high, high], axis=1) for high, rest in parts]
    a_low = [rest for high, rest in parts]
    for c in range(0, 2 * cols, WIDTH):
        here = pl.ds(c, WIDTH)
        total = three(
            a_high, a_low, [both[k, :, here] for k in at], [both[k, :bs, here] for k in at]
        )
        result[here, :] = total.T
    for n in range(count):

        @pl.when(g == n)
        def _(n=n):
            outs[n][...] = result[...]


def parts_kernel(own, other, out):
    blocks, _, bs, _ = own.shape
    for k, trans in enumerate((own, other)):
        for i in range(blocks):
            for t in range(BAND):
                high, rest = split(trans[i, t])
                out[k, i, t, :, :bs] = high
                out[k, i, t, :, bs:] = rest


def step_kernel(halves, finish, merge, others, passed, rows, meta, band, other_band, parts, noise, *refs):
    refs = list(refs)
    take = lambda count: [refs.pop(0) for _ in range(count)]
    pieces = [take(3) for _ in finish]
    got = take(len(merge))
    take(others)
    out = refs.pop(0) if 0 in halves or merge else None
    give = refs.pop(0) if 1 in halves else None
    take(passed)
    side, core = meta[1], meta[2]
    ends = []

    def column(place, width):
        return pl.ds(pl.multiple_of(row_at(meta, rows, place) * width, width), width)

    def end(copy):
        copy.start()
        ends.append(copy)

    if finish:
        tiles, both, weights, added, result, sems, weight_sems, out_sems = take(8)
        _, blocks, _, bs, _ = weights.shape
        reads = [
            [pltpu.make_async_copy(pieces[f][k], tiles.at[f, k], sems.at[f, k]) for k in range(3)]
            for f in range(len(finish))
        ]
        here = [column(2 * n + core, bs) for n in finish]
        adds = [
            pltpu.make_async_copy(noise.at[:, here[f]], added.at[f], sems.at[f, 3])
            for f in range(len(finish))
            if 0 in halves
        ]
        loads = {
            k: [
                pltpu.make_async_copy(parts.at[k, i], weights.at[k, i], weight_sems.at[k, i])
                for i in range(blocks)
            ]
            for k in halves
        }
        for copy in sum(reads[:2] + [loads[k] for k in halves] + reads[2:], []) + adds:
            copy.start()
    merges = []
    for m, chunks in enumerate(merge):
        sums, got_tile, merge_sems = take(3)
        width = got_tile.shape[1] // len(chunks)
        there = [column(2 * n + 1 - core, width) for n in chunks]
        copies = [pltpu.make_async_copy(got[m], got_tile, merge_sems.at[0, 0])]
        for k in range(len(chunks)):
            copies.append(
                pltpu.make_async_copy(noise.at[:, there[k]], sums.at[k], merge_sems.at[1, k])
            )
        for copy in copies:
            copy.start()
        merges.append((copies, sums, got_tile, merge_sems, there, width))
    if finish:
        chip = tiles.shape[2] // bs
        base = (meta[3] // 2 - 1) * chip
        lanes = both.shape[3] // bs
        for first in range(0, len(finish), lanes):
            now = both.at[first // lanes % both.shape[0]]
            for f in range(first, first + lanes):
                to = slice((f - first) * bs, (f - first + 1) * bs)
                for k, slot in enumerate((1, 2 - 2 * side, 2 * side)):
                    reads[f][k].wait()
                    for b in range(chip):
                        high, rest = split(tiles[f, k, b * bs : (b + 1) * bs, :])
                        now[slot * chip + b, :bs, to] = high
                        now[slot * chip + b, bs:, to] = rest
            for k in halves:
                table = other_band if k else band
                for i in range(blocks):
                    if first == 0:
                        loads[k][i].wait()
                    at = [table[i, t] - base for t in range(BAND)]
                    highs = [weights[k, i, t, :, :bs] for t in range(BAND)]
                    result[k, i * bs : (i + 1) * bs, first * bs : (first + lanes) * bs] = three(
                        [jnp.concatenate([high, high], axis=1) for high in highs],
                        [weights[k, i, t, :, bs:] for t in range(BAND)],
                        [now[j] for j in at],
                        [now[j, :bs, :] for j in at],
                    )
        end(pltpu.make_async_copy(result.at[1], give, out_sems.at[0]))
        for f in range(len(adds)):
            adds[f].wait()
            added[f] = added[f] + result[0, :, f * bs : (f + 1) * bs]
            end(pltpu.make_async_copy(added.at[f], out.at[:, here[f]], out_sems.at[1 + f]))
    for copies, sums, got_tile, merge_sems, there, width in merges:
        for copy in copies:
            copy.wait()
        for k in range(len(there)):
            sums[k] = sums[k] + got_tile[:, k * width : (k + 1) * width]
            end(pltpu.make_async_copy(sums.at[k], out.at[:, there[k]], merge_sems.at[2, k]))
    for copy in ends:
        copy.wait()


ANY = pl.BlockSpec(memory_space=pl.ANY)
SMEM = pl.BlockSpec(memory_space=pltpu.SMEM)
VMEM = pl.BlockSpec(memory_space=pltpu.VMEM)
DMA = pltpu.SemaphoreType.DMA


def params():
    return pltpu.CompilerParams(vmem_limit_bytes=63 * 1024 * 1024)


def cost(rows, depth, cols, moved):
    return pl.CostEstimate(
        flops=6 * rows * depth * cols, bytes_accessed=4 * moved, transcendentals=0
    )


def rows_of(state, meta, bs, place, count, after):
    edge = (count * bs, state.shape[1])
    return pl.pallas_call(
        functools.partial(rows_kernel, place, bs),
        out_shape=jax.ShapeDtypeStruct(edge, state.dtype),
        in_specs=[SMEM, ANY, ANY],
        out_specs=ANY,
        scratch_shapes=[pltpu.VMEM(edge, state.dtype), DMA((2, count))],
        compiler_params=params(),
        name="rows",
    )(meta, state, after)


def first_stage(trans, band, meta, state, near, whole, halos, start, count, beyond, after):
    band_rows, _, bs, _ = trans.shape
    cols = state.shape[1]
    window = 2 * count + 2 * REACH - 1

    def mine(g, band, meta):
        return (row_at(meta, band_rows, 2 * (start + g) + meta[2]), 0, 0, 0)

    return pl.pallas_call(
        functools.partial(first_kernel, start, count, beyond, len(after)),
        out_shape=[jax.ShapeDtypeStruct((2 * cols, bs), jnp.float32)] * count,
        grid_spec=pltpu.PrefetchScalarGridSpec(
            num_scalar_prefetch=2,
            grid=(count,),
            in_specs=[pl.BlockSpec((1, BAND, bs, bs), mine)] + [ANY] * (5 + len(after)),
            out_specs=[pl.BlockSpec((2 * cols, bs), lambda g, band, meta: (0, 0))] * count,
            scratch_shapes=[
                pltpu.VMEM((2, window, bs, cols), jnp.float32),
                pltpu.VMEM((window, 2 * bs, 2 * cols), jnp.bfloat16),
                pltpu.VMEM((2 * cols, bs), jnp.float32),
                DMA((2, window)),
            ],
        ),
        compiler_params=params(),
        cost_estimate=cost(count * bs, BAND * bs, 2 * cols, count * bs * (BAND * bs + 18 * cols)),
        name="first",
    )(band, meta, trans, state, near, whole, *halos, *after)


def parts_of(own, other, after):
    blocks, band, bs, _ = own.shape
    return pl.pallas_call(
        lambda own, other, after, out: parts_kernel(own, other, out),
        out_shape=jax.ShapeDtypeStruct((2, blocks, band, bs, 2 * bs), jnp.bfloat16),
        in_specs=[VMEM, VMEM, ANY],
        out_specs=VMEM,
        compiler_params=params(),
        cost_estimate=cost(1, 1, 1, 4 * own.size),
        name="parts",
    )(own, other, after)


def step(meta, bands, parts, noise, halves, finish, merge, out, passed, after):
    blocks, bs = parts.shape[-4], parts.shape[-2]
    rows = noise.shape[1] // bs
    operands = [x for one in finish for x in one[1:]] + [one[1] for one in merge]
    others = list(after)
    shapes, aliases = [], {}
    if 0 in halves or merge:
        if out is not None:
            aliases[5 + len(operands) + len(others)] = 0
            others.append(out)
        shapes.append(jax.ShapeDtypeStruct(noise.shape, noise.dtype))
    scratch = []
    column = (noise.shape[0], bs)
    if finish:
        count = len(finish)
        wide = (noise.shape[0], count * bs)
        if 1 in halves:
            shapes.append(jax.ShapeDtypeStruct(wide, noise.dtype))
        tile = finish[0][1].shape
        scratch += [
            pltpu.VMEM((count, 3, *tile), jnp.float32),
            pltpu.VMEM((-(-count // 2), 3 * tile[0] // bs, 2 * bs, min(count, 2) * bs), jnp.bfloat16),
            pltpu.VMEM(parts.shape, parts.dtype),
            pltpu.VMEM((count, *column), jnp.float32),
            pltpu.VMEM((2, *wide), jnp.float32),
            DMA((count, 4)),
            DMA((2, blocks)),
            DMA((1 + count,)),
        ]
    for chunks, got in merge:
        count = len(chunks)
        scratch += [
            pltpu.VMEM((count, *column), jnp.float32),
            pltpu.VMEM(got.shape, jnp.float32),
            DMA((3, count)),
        ]
    for x in passed:
        aliases[5 + len(operands) + len(others)] = len(shapes)
        others.append(x)
        shapes.append(jax.ShapeDtypeStruct(x.shape, x.dtype))
    got = list(
        pl.pallas_call(
            functools.partial(
                step_kernel, halves, [one[0] for one in finish], [one[0] for one in merge],
                len(others), len(passed), rows,
            ),
            out_shape=shapes,
            in_specs=[SMEM] * 3 + [ANY] * (2 + len(operands) + len(others)),
            out_specs=[ANY] * len(shapes),
            scratch_shapes=scratch,
            input_output_aliases=aliases,
            compiler_params=params(),
            cost_estimate=cost(2 * blocks * bs, BAND * bs, bs, parts.size),
            name="step",
        )(meta, *bands, parts, noise, *operands, *others)
    )
    out = got.pop(0) if 0 in halves or merge else out
    give = got.pop(0) if 1 in halves else None
    return out, give, got


def paired(state_cov, trans_first, band_first, trans_second, band_second, noise_cov):
    band_rows, bs = trans_first.shape[0], trans_first.shape[2]
    count = lax.axis_size("col")
    here = lax.axis_index("col")
    meta = jnp.stack([lax.axis_index("row"), here // 2 % 2, here % 2, here]).astype(jnp.int32)
    devices = range(count)
    to_other = [(c, c ^ 1) for c in devices]
    to_pair = [(c, c ^ 2) for c in devices]
    to_far = [(c, c + (4 if c & 2 == 0 else -4)) for c in devices]
    to_far = [(c, d) for c, d in to_far if 0 <= d < count]
    chunks = band_rows // 2
    swap = lambda x: lax.ppermute(x, "col", to_other)
    own, pair, far = [], [], []
    halos = (state_cov, state_cov)
    out = None

    def first(after):
        start = len(own)
        size = FIRST[sum(1 for k in range(len(FIRST)) if sum(FIRST[: k + 1]) <= start)]
        beyond = 2 * (start + size) + REACH > band_rows
        own.extend(
            first_stage(
                trans_first, band_first, meta, state_cov, near, whole if start > 1 else near, halos,
                start, size, beyond, after,
            )
        )
        return [own[-1]]

    def send(x):
        pair.append(lax.ppermute(x, "col", to_pair))

    rows = lambda place, size, after: rows_of(state_cov, meta, bs, place, size, after)
    ahead = rows(0, NEAR, meta)
    near = swap(ahead)
    edge = rows(band_rows - REACH, REACH, ahead)
    halo = lax.ppermute(edge, "row", [(0, 1), (1, 0)])
    tile, near = lax.optimization_barrier((state_cov, near))
    whole = swap(tile)
    bands = (band_second, swap(band_second))
    last = first([edge])
    send(own[0])
    trans, last[0] = lax.optimization_barrier((trans_second, last[0]))
    last = first([*last, bands[1]])
    send(own[1])
    other_trans = swap(trans)
    if PARTS < 0:
        parts = parts_of(trans_second, other_trans, last[0])
        last = [parts]
    last = first(last)
    gave, merge = [], []
    if PARTS >= 0:
        parts = trans_second

    def finish(first_chunk, size):
        nonlocal out, last, merge
        done = tuple(range(first_chunk, first_chunk + size))
        out, give, _ = step(
            meta, bands, parts, noise_cov, (1, 0),
            [(m, own[m], pair[m], far[m]) for m in done], merge, out, [], [x for x in last if x is not out],
        )
        gave.append((done, swap(give)))
        merge = []
        last = [out]

    for n in range(chunks + 2):
        if n < chunks:
            after = [far[n - 2]] if n >= 2 else []
            passed = [pair[n]]
            if n + 2 < chunks:
                passed.append(own[n + 2])
            if n == HALO:
                passed.append(halo)
            _, _, got = step(
                meta, bands, parts, noise_cov, (), [], [], None, passed, [*last, *after]
            )
            pair[n], last = got[0], got[:1]
            if n == HALO:
                halos = (got[-1], swap(got[-1]))
            if n + 2 < chunks:
                own[n + 2] = got[1]
                send(own[n + 2])
            far.append(lax.ppermute(pair[n], "col", to_far))
            if n in FIRSTS:
                last = first(last)
            if n == PARTS:
                parts = parts_of(trans_second, other_trans, last[0])
                last = [parts]
        for at, first_chunk, size in FINISH:
            if at == n:
                if n in MERGE:
                    merge, gave = gave, []
                finish(first_chunk, size)
    out, _, _ = step(meta, bands, parts, noise_cov, (), [], gave, out, [], [])
    return out


def solution(mesh):
    def whole(state_cov, trans_first, band_first, trans_second, band_second, noise_cov):
        band_rows, bs = trans_first.shape[0], trans_first.shape[2]
        chip = 2 * state_cov.shape[1]
        fits = (
            mesh.shape["row"] == 2
            and mesh.shape["col"] % 4 == 0
            and band_rows >= 4 * REACH
            and chip == REACH * bs
            and band_rows == 2 * sum(FIRST) == 2 * sum(size for _, _, size in FINISH)
        )
        do = paired if fits else body
        return do(state_cov, trans_first, band_first, trans_second, band_second, noise_cov)

    return jax.shard_map(
        whole,
        mesh=mesh,
        in_specs=(
            P("row", "col"),
            P("row", None, None, None),
            P("row", None),
            P("col", None, None, None),
            P("col", None),
            P("col", "row"),
        ),
        out_specs=P("col", "row"),
        check_vma=False,
    )
```
